32 devices in a mesh: grp: 2 (over y), chain: 16 (over z, x, core).
Axes of the slice: x: 2, y: 2, z: 4, core: 2. Of those that a mesh axis runs over, the one named last changes fastest.
Arguments:
- left_env: bfloat16 [2048, 128, 128], P(('grp', 'chain')), parts along dimension 0, may hold values from -40 to 40
- site_tensor: bfloat16 [2048, 128, 128], P(('grp', 'chain')), parts along dimension 0, may hold values from -0.5 to 0.5
- right_env: bfloat16 [2048, 128, 128], P(('grp', 'chain')), parts along dimension 0, may hold values from -0.5 to 0.5
- center: bfloat16 [2048, 128, 128], P(('grp', 'chain')), parts along dimension 0, may hold values from -0.5 to 0.5
- mpo_table: float32 [10816], replicated, may hold values from -4 to 4
- update_terms: int32 [8192, 5], P(('grp', 'chain')), parts along dimension 0, may hold values from 0 to 10815, as said below
- update_count: int32 [32], P(('grp', 'chain')), parts along dimension 0, may hold values from 64 to 256, as said below
- heff_terms: int32 [8192, 6], P(('grp', 'chain')), parts along dimension 0, may hold values from 0 to 10815, as said below
- heff_count: int32 [32], P(('grp', 'chain')), parts along dimension 0, may hold values from 64 to 256, as said below
Outputs:
- product: bfloat16 [2048, 128, 128], P(('grp', 'chain')), parts along dimension 0
- log_scale: float32 [32], P(('grp', 'chain')), parts along dimension 0
The draws below stay inside these ranges and needn't reach their ends.
There are 2 independent parts, one for each index of `grp`. The reference program is written for one: setup_inputs(seed, part) draws one part's arguments, and reference() takes and returns one part's arrays. A program takes and returns all parts, laid end to end along the dimension named above; an argument that names none is the same for every part. Nothing has to cross between parts.
Inputs may be any that keep to these rules, and one draw needn't show every extreme that they name: `update_terms`: columns hold indices below 64, 64, 64, 64, 10816 in that order. `heff_terms`: columns hold indices below 64, 64, 64, 64, 10816, 10816 in that order. `update_count`: some segment uses all 256 slots. `heff_count`: some segment uses all 256 slots.
All inputs are finite; a program needn't handle non-finite values.
Results may differ from the reference program's by a relative error of at most 0.0072.
Values may be sent and summed in bfloat16 or wider, within the bound.
A program may use at most 128 MiB of HBM per device.

```python
import jax
import jax.numpy as jnp
from jax import lax

SECTOR = 128
BLOCKS = 64
UPD_TERMS = 256
HEFF_TERMS = 256
MPO_ENTRIES = 10816
N_CHAIN = 16


def draw_left_env(key, part):
    key = jax.random.fold_in(key, 11)
    total = N_CHAIN * BLOCKS
    place = jnp.arange(total, dtype=jnp.float32) / max(total - 1, 1)
    scale = 2.0 * jnp.power(3.0, place)
    first = jax.random.fold_in(key, 0)
    base = jnp.clip(jax.random.normal(first, (total, SECTOR, SECTOR), jnp.float32), -6.0, 6.0)
    return (base * scale[:, None, None]).astype(jnp.bfloat16)


def term_list(key, rows, limits):
    raw = jax.random.randint(key, (rows, len(limits)), 0, 1 << 30)
    return raw % jnp.array(limits, dtype=jnp.int32)[None, :]


def draw_update_terms(key, part):
    key = jax.random.fold_in(key, 21)
    return term_list(key, N_CHAIN * UPD_TERMS, [BLOCKS, BLOCKS, BLOCKS, BLOCKS, MPO_ENTRIES])


def draw_heff_terms(key, part):
    key = jax.random.fold_in(key, 31)
    return term_list(key, N_CHAIN * HEFF_TERMS, [BLOCKS, BLOCKS, BLOCKS, BLOCKS, MPO_ENTRIES, MPO_ENTRIES])


def live_counts(key, capacity):
    first, second = jax.random.split(key)
    counts = jax.random.randint(first, (N_CHAIN,), capacity // 4, capacity // 2 + 1)
    busiest = jax.random.randint(second, (), 0, N_CHAIN)
    return jnp.where(jnp.arange(N_CHAIN) == busiest, capacity, counts).astype(jnp.int32)


def draw_update_count(key, part):
    key = jax.random.fold_in(key, 41)
    return live_counts(key, UPD_TERMS)


def draw_heff_count(key, part):
    key = jax.random.fold_in(key, 51)
    return live_counts(key, HEFF_TERMS)


def block_scale(rng, dims, cuts, smallest, largest):
    factor_of, own = 1.0, jax.random.fold_in(rng, 6)
    for axis_at, shards_of in cuts:
        steps = jnp.exp(jax.random.uniform(jax.random.fold_in(own, axis_at), (shards_of,), jnp.float32, smallest / len(cuts), largest / len(cuts)))
        factor_of = factor_of * jnp.repeat(steps, dims[axis_at] // shards_of).reshape([-1 if axis == axis_at else 1 for axis in range(len(dims))])
    return factor_of


def normal_values(stream_key, dims, deviation, most, cuts=(), held_as=jnp.bfloat16):
    entries = jax.random.normal(stream_key, dims, jnp.float32) * deviation
    if len(cuts) > 0:
        entries = block_scale(stream_key, dims, cuts, -0.22, 0.18) * entries
    return jnp.clip(entries, min=-most, max=most).astype(held_as)


def setup_inputs(seed: int = 0, part: int = 0) -> dict:
    arg_keys = jax.random.split(jax.random.key(seed), 10)
    part_keys = jax.random.split(jax.random.fold_in(arg_keys[9], part), 10)
    left_env = draw_left_env(jax.random.fold_in(jax.random.fold_in(arg_keys[9], part), 71), part)
    site_tensor = normal_values(part_keys[1], (N_CHAIN * BLOCKS, SECTOR, SECTOR), SECTOR ** -0.5, 0.5, ((0, 16),))
    right_env = normal_values(part_keys[2], (N_CHAIN * BLOCKS, SECTOR, SECTOR), SECTOR ** -0.5, 0.5, ((0, 16),))
    center = normal_values(part_keys[3], (N_CHAIN * BLOCKS, SECTOR, SECTOR), SECTOR ** -0.5, 0.5, ((0, 16),))
    mpo_table = normal_values(arg_keys[4], (MPO_ENTRIES,), 1.0, 4.0, (), jnp.float32)
    update_terms = draw_update_terms(jax.random.fold_in(jax.random.fold_in(arg_keys[9], part), 71), part)
    update_count = draw_update_count(jax.random.fold_in(jax.random.fold_in(arg_keys[9], part), 71), part)
    heff_terms = draw_heff_terms(jax.random.fold_in(jax.random.fold_in(arg_keys[9], part), 71), part)
    heff_count = draw_heff_count(jax.random.fold_in(jax.random.fold_in(arg_keys[9], part), 71), part)
    return {"left_env": left_env, "site_tensor": site_tensor, "right_env": right_env, "center": center, "mpo_table": mpo_table, "update_terms": update_terms, "update_count": update_count, "heff_terms": heff_terms, "heff_count": heff_count}


def contract_update(blocks_env, blocks_site, terms, count, mpo_table):
    live = jnp.arange(terms.shape[0]) < count
    coef = jnp.where(live, mpo_table[terms[:, 4]], jnp.zeros((), mpo_table.dtype)).astype(jnp.float32)
    left = blocks_env[terms[:, 0]].astype(jnp.float32)
    upper = blocks_site[terms[:, 1]].astype(jnp.float32)
    lower = blocks_site[terms[:, 2]].astype(jnp.float32)
    part = jnp.einsum('tij,tik->tjk', upper, left).astype(jnp.bfloat16)
    part = lax.optimization_barrier(part).astype(jnp.float32)
    full = jnp.einsum('tjk,tkl->tjl', part, lower) * coef[:, None, None]
    summed = jax.ops.segment_sum(full, terms[:, 3], num_segments=blocks_env.shape[0])
    return summed.astype(jnp.bfloat16)

def contract_heff(normed, blocks_center, blocks_right, terms, count, mpo_table):
    live = jnp.arange(terms.shape[0]) < count
    both = mpo_table[terms[:, 4]] * mpo_table[terms[:, 5]]
    coef = jnp.where(live, both, jnp.zeros((), both.dtype)).astype(jnp.float32)
    waves = blocks_center[terms[:, 1]].astype(jnp.float32)
    rights = blocks_right[terms[:, 2]].astype(jnp.float32)
    half = jnp.einsum('tij,tjk->tik', waves, rights).astype(jnp.bfloat16)
    half = lax.optimization_barrier(half).astype(jnp.float32)
    lefts = normed[terms[:, 0]].astype(jnp.float32)
    full = jnp.einsum('tji,tjk->tik', lefts, half) * coef[:, None, None]
    summed = jax.ops.segment_sum(full, terms[:, 3], num_segments=blocks_center.shape[0])
    return summed.astype(jnp.bfloat16)

def reference(left_env, site_tensor, right_env, center, mpo_table, update_terms, update_count, heff_terms, heff_count):
    shape4 = (N_CHAIN, BLOCKS, SECTOR, SECTOR)
    left4 = left_env.reshape(shape4)
    site4 = site_tensor.reshape(shape4)
    right4 = right_env.reshape(shape4)
    center4 = center.reshape(shape4)
    uterms = update_terms.reshape(N_CHAIN, UPD_TERMS, 5)
    hterms = heff_terms.reshape(N_CHAIN, HEFF_TERMS, 6)
    fresh = lax.map(lambda item: contract_update(item[0], item[1], item[2], item[3], mpo_table), (left4, site4, uterms, update_count))
    seam = jnp.concatenate([left4[:1], fresh[:-1]], axis=0)
    seam32 = seam.astype(jnp.float32)
    scale = jnp.sqrt(lax.optimization_barrier(jnp.mean(seam32 * seam32, axis=(1, 2, 3))) + 1e-06)
    log_scale = jnp.cumsum(jnp.log(scale))
    normed = (seam32 / scale[:, None, None, None]).astype(jnp.bfloat16)
    product = lax.map(lambda item: contract_heff(item[0], item[1], item[2], item[3], item[4], mpo_table), (normed, center4, right4, hterms, heff_count))
    return (product.reshape(N_CHAIN * BLOCKS, SECTOR, SECTOR), log_scale)
```

```python
import jax
import jax.numpy as jnp
from jax import lax
from jax.experimental import pallas as pl
from jax.experimental.pallas import tpu as pltpu
from jax.sharding import PartitionSpec as P

UNROLL = 8
GROUP = 32
VMEM_LIMIT = 48 * 1024 * 1024


def dot(a, b):
    return jnp.dot(a, b, preferred_element_type=jnp.float32)


def dot_t(a, b):
    return lax.dot_general(a, b, (((1,), (1,)), ((), ())), preferred_element_type=jnp.float32)


def update_kernel(place, count, terms, table, left, site, fresh, squares, site_t, acc):
    blocks = left.shape[0]

    def prepare(k, carry):
        site_t[k] = site[k].T
        acc[k] = jnp.zeros(acc.shape[1:], jnp.float32)
        return carry

    lax.fori_loop(0, blocks, prepare, 0, unroll=4)
    live = count[0]

    def advance(g, carry):
        sums = []
        for u in range(UNROLL):
            t = g * UNROLL + u
            coef = jnp.where(t < live, table[terms[4, t]], 0.0)
            part = dot(site_t[terms[1, t]], left[terms[0, t]]).astype(jnp.bfloat16)
            full = dot_t(site_t[terms[2, t]], part)
            sums.append((terms[3, t], full * coef))
        for o, full in sums:
            acc[o] += full
        return carry

    lax.fori_loop(0, (live + UNROLL - 1) // UNROLL, advance, 0)

    def finish(k, total):
        rounded = acc[k].astype(jnp.bfloat16)
        fresh[k] = rounded
        wide = rounded.astype(jnp.float32)
        return total + wide * wide

    zero = jnp.zeros(acc.shape[1:], jnp.float32)
    squares[0] = jnp.sum(lax.fori_loop(0, blocks, finish, zero, unroll=4))
    squares[1] = 0.0

    @pl.when(place[0] == 0)
    def _():
        def add(k, total):
            wide = left[k].astype(jnp.float32)
            return total + wide * wide

        squares[1] = jnp.sum(lax.fori_loop(0, blocks, add, zero, unroll=4))


def half_kernel(count, terms, center, right, half):
    base = pl.program_id(0) * GROUP

    @pl.when(base < count[0])
    def _():
        for u in range(GROUP):
            t = base + u
            half[u] = dot(center[terms[1, t]], right[terms[2, t]]).astype(jnp.bfloat16)


def product_kernel(count, terms, place, table, scale, half, left, incoming, product, seam, acc, sem):
    step = pl.program_id(0)
    base = step * GROUP
    blocks = acc.shape[0]
    live = count[0]

    @pl.when(step == 0)
    def _():
        @pl.when(place[0] != 0)
        def _():
            copy = pltpu.make_async_copy(incoming, seam, sem)
            copy.start()
            copy.wait()

        @pl.when(place[0] == 0)
        def _():
            copy = pltpu.make_async_copy(left, seam, sem)
            copy.start()
            copy.wait()

            def turn(k, carry):
                seam[k] = seam[k].T
                return carry

            lax.fori_loop(0, blocks, turn, 0, unroll=4)

        def clear(k, carry):
            acc[k] = jnp.zeros(acc.shape[1:], jnp.float32)
            return carry

        lax.fori_loop(0, blocks, clear, 0, unroll=4)

    @pl.when(base < live)
    def _():
        def advance(g, carry):
            sums = []
            for u in range(UNROLL):
                k = g * UNROLL + u
                t = base + k
                coef = jnp.where(t < live, table[terms[4, t]] * table[terms[5, t]], 0.0)
                sums.append((terms[3, t], dot(seam[terms[0, t]], half[k]) * coef))
            for o, full in sums:
                acc[o] += full
            return carry

        lax.fori_loop(0, GROUP // UNROLL, advance, 0)

    @pl.when(step == pl.num_programs(0) - 1)
    def _():
        def finish(k, carry):
            product[k] = (acc[k] / scale[0]).astype(jnp.bfloat16)
            return carry

        lax.fori_loop(0, blocks, finish, 0, unroll=4)


def smem():
    return pl.BlockSpec(memory_space=pltpu.SMEM)


def vmem():
    return pl.BlockSpec(memory_space=pltpu.VMEM)


def per_device(
    left_env,
    site_tensor,
    right_env,
    center,
    mpo_table,
    update_terms,
    update_count,
    heff_terms,
    heff_count,
):
    chain, mine = lax.axis_size("chain"), lax.axis_index("chain")
    place = mine.reshape(1).astype(jnp.int32)
    blocks, rows, cols = left_env.shape
    slots = heff_terms.shape[0]
    update_terms, heff_terms = update_terms.T, heff_terms.T
    params = pltpu.CompilerParams(vmem_limit_bytes=VMEM_LIMIT)

    fresh, squares = pl.pallas_call(
        update_kernel,
        out_shape=(
            jax.ShapeDtypeStruct(left_env.shape, jnp.bfloat16),
            jax.ShapeDtypeStruct((2,), jnp.float32),
        ),
        in_specs=[smem(), smem(), smem(), smem(), vmem(), vmem()],
        out_specs=(vmem(), smem()),
        scratch_shapes=[
            pltpu.VMEM((blocks, cols, rows), jnp.bfloat16),
            pltpu.VMEM((blocks, cols, cols), jnp.float32),
        ],
        compiler_params=params,
        cost_estimate=pl.CostEstimate(flops=10**9, bytes_accessed=6 * 2**20, transcendentals=0),
        name="update",
    )(place, update_count, update_terms, mpo_table, left_env, site_tensor)

    incoming = lax.ppermute(fresh, "chain", [(k, k + 1) for k in range(chain - 1)])
    gathered = lax.all_gather(squares, "chain")

    def current(step, count, *rest):
        return (jnp.minimum(step, (count[0] - 1) // GROUP), 0, 0)

    half = pl.pallas_call(
        half_kernel,
        out_shape=jax.ShapeDtypeStruct((slots,) + center.shape[1:], jnp.bfloat16),
        grid_spec=pltpu.PrefetchScalarGridSpec(
            num_scalar_prefetch=2,
            grid=(slots // GROUP,),
            in_specs=[vmem(), vmem()],
            out_specs=pl.BlockSpec((GROUP, rows, cols), current),
        ),
        compiler_params=params,
        cost_estimate=pl.CostEstimate(flops=10**9, bytes_accessed=8 * 2**20, transcendentals=0),
        name="half",
    )(heff_count, heff_terms, center, right_env)

    scales = jnp.sqrt(gathered / left_env.size + 1e-06)
    logs = jnp.log(scales)
    before = jnp.where(jnp.arange(chain) < mine, logs[:, 0], 0.0)
    log_scale = (logs[0, 1] + jnp.sum(before)).reshape(1)
    from_left = jnp.sum(jnp.where(jnp.arange(chain) == mine - 1, scales[:, 0], 0.0))
    scale = jnp.where(mine == 0, scales[0, 1], from_left).reshape(1)

    product = pl.pallas_call(
        product_kernel,
        out_shape=jax.ShapeDtypeStruct(center.shape, jnp.bfloat16),
        grid_spec=pltpu.PrefetchScalarGridSpec(
            num_scalar_prefetch=2,
            grid=(slots // GROUP,),
            in_specs=[
                smem(),
                smem(),
                smem(),
                pl.BlockSpec((GROUP, rows, cols), current),
                pl.BlockSpec(memory_space=pl.ANY),
                pl.BlockSpec(memory_space=pl.ANY),
            ],
            out_specs=vmem(),
            scratch_shapes=[
                pltpu.VMEM(left_env.shape, jnp.bfloat16),
                pltpu.VMEM(center.shape, jnp.float32),
                pltpu.SemaphoreType.DMA,
            ],
        ),
        compiler_params=params,
        name="product",
    )(heff_count, heff_terms, place, mpo_table, scale, half, left_env, incoming)
    return (product, log_scale)


def solution(mesh):
    placed = (
        P(("grp", "chain"), None, None),
        P(("grp", "chain"), None, None),
        P(("grp", "chain"), None, None),
        P(("grp", "chain"), None, None),
        P(),
        P(("grp", "chain"), None),
        P(("grp", "chain")),
        P(("grp", "chain"), None),
        P(("grp", "chain")),
    )
    return jax.shard_map(
        per_device,
        mesh=mesh,
        in_specs=placed,
        out_specs=(P(("grp", "chain"), None, None), P(("grp", "chain"))),
        check_vma=False,
    )
```

```python
import jax
import jax.numpy as jnp
from jax import lax
from jax.experimental import pallas as pl
from jax.experimental.pallas import tpu as pltpu
from jax.sharding import PartitionSpec as P

UNROLL = 8
GROUP = 32
VMEM_LIMIT = 48 * 1024 * 1024
TILE = (8, 128)


def dot(a, b):
    return jnp.dot(a, b, preferred_element_type=jnp.float32)


def update_kernel(place, count, terms, table, left, site, fresh, squares, site_t, parts, acc):
    blocks = left.shape[0]

    def prepare(k, carry):
        site_t[k] = site[k].T
        acc[k] = jnp.zeros(acc.shape[1:], jnp.float32)
        return carry

    lax.fori_loop(0, blocks, prepare, 0, unroll=4)
    live = count[0]
    groups = (live + UNROLL - 1) // UNROLL

    def first(g, carry):
        for u in range(UNROLL):
            t = g * UNROLL + u
            coef = jnp.where(t < live, table[terms[4, t]], 0.0)
            part = dot(site_t[terms[1, t]], left[terms[0, t]]) * coef
            parts[t] = part.astype(jnp.bfloat16)
        return carry

    lax.fori_loop(0, groups, first, 0)

    def second(g, carry):
        sums = []
        for u in range(UNROLL):
            t = g * UNROLL + u
            sums.append((terms[3, t], dot(parts[t], site[terms[2, t]])))
        for o, full in sums:
            acc[o] += full
        return carry

    lax.fori_loop(0, groups, second, 0)

    def finish(k, total):
        rounded = acc[k].astype(jnp.bfloat16)
        fresh[k] = rounded.T
        wide = rounded.astype(jnp.float32)
        return total + wide * wide

    zero = jnp.zeros(acc.shape[1:], jnp.float32)
    total = lax.fori_loop(0, blocks, finish, zero, unroll=4)
    squares[...] = jnp.full(TILE, jnp.sum(total))

    @pl.when(place[0] == 0)
    def _():
        def add(k, total):
            wide = left[k].astype(jnp.float32)
            return total + wide * wide

        total = lax.fori_loop(0, blocks, add, zero, unroll=4)
        squares[1:, :] = jnp.full((TILE[0] - 1, TILE[1]), jnp.sum(total))


def half_kernel(count, terms, table, center, right, squares, half, passed):
    base = pl.program_id(0) * GROUP
    passed[...] = squares[...]

    @pl.when(base < count[0])
    def _():
        for u in range(GROUP):
            t = base + u
            coef = jnp.where(t < count[0], table[terms[4, t]] * table[terms[5, t]], 0.0)
            value = dot(center[terms[1, t]], right[terms[2, t]]) * coef
            half[u] = value.astype(jnp.bfloat16)


def exchange_kernel(size, squares, log_scale, scale, held, send_sem, recv_sem):
    chain, mine = held.shape[0], lax.axis_index("chain")
    held[...] = jnp.zeros(held.shape, jnp.float32)
    held[mine] = squares[...]
    barrier = pltpu.get_barrier_semaphore()

    def copy(source, target):
        return pltpu.make_async_remote_copy(
            src_ref=squares,
            dst_ref=held.at[source],
            send_sem=send_sem.at[target],
            recv_sem=recv_sem.at[source],
            device_id={"chain": target},
            device_id_type=pl.DeviceIdType.MESH,
        )

    def greet(k, carry):
        @pl.when(k != mine)
        def _():
            pl.semaphore_signal(
                barrier, inc=1, device_id={"chain": k}, device_id_type=pl.DeviceIdType.MESH
            )

        return carry

    lax.fori_loop(0, chain, greet, 0)
    pl.semaphore_wait(barrier, chain - 1)

    def send(k, carry):
        copy(mine, k).start()
        return carry

    def sent(k, carry):
        copy(mine, k).wait_send()
        return carry

    def arrived(k, carry):
        copy(k, mine).wait_recv()
        return carry

    lax.fori_loop(mine + 1, chain, send, 0)
    lax.fori_loop(0, mine, arrived, 0)
    lax.fori_loop(mine + 1, chain, sent, 0)
    scales = jnp.sqrt(held[...] / size + 1e-06)
    logs = jnp.log(scales)
    segment = lax.broadcasted_iota(jnp.int32, held.shape, 0)
    row = lax.broadcasted_iota(jnp.int32, held.shape, 1)
    lane = lax.broadcasted_iota(jnp.int32, held.shape, 2)
    opening = (segment == 0) & (row == 1)
    passed = (segment < mine) & (row == 0)
    log_scale[0] = jnp.sum(jnp.where((opening | passed) & (lane == 0), logs, 0.0))
    behind = (segment == jnp.maximum(mine - 1, 0)) & (row == jnp.where(mine == 0, 1, 0))
    scale[0] = jnp.sum(jnp.where(behind & (lane == 0), scales, 0.0))


def product_kernel(count, terms, place, scale, half, left, incoming, product, seam, acc, sem):
    step = pl.program_id(0)
    base = step * GROUP
    blocks = acc.shape[0]

    @pl.when(step == 0)
    def _():
        source = [left, incoming]
        for index in range(2):

            @pl.when((place[0] != 0) == (index == 1))
            def _():
                pltpu.make_async_copy(source[index], seam, sem).start()

        def clear(k, carry):
            acc[k] = jnp.zeros(acc.shape[1:], jnp.float32)
            return carry

        lax.fori_loop(0, blocks, clear, 0, unroll=4)
        pltpu.make_async_copy(incoming, seam, sem).wait()

        @pl.when(place[0] == 0)
        def _():
            def turn(k, carry):
                seam[k] = seam[k].T
                return carry

            lax.fori_loop(0, blocks, turn, 0, unroll=4)

    @pl.when(base < count[0])
    def _():
        def advance(g, carry):
            sums = []
            for u in range(UNROLL):
                k = g * UNROLL + u
                t = base + k
                sums.append((terms[3, t], dot(seam[terms[0, t]], half[k])))
            for o, full in sums:
                acc[o] += full
            return carry

        lax.fori_loop(0, GROUP // UNROLL, advance, 0)

    @pl.when(step == pl.num_programs(0) - 1)
    def _():
        inverse = 1.0 / jnp.full((1, acc.shape[2]), scale[0])

        def finish(k, carry):
            product[k] = (acc[k] * inverse).astype(jnp.bfloat16)
            return carry

        lax.fori_loop(0, blocks, finish, 0, unroll=4)


def smem():
    return pl.BlockSpec(memory_space=pltpu.SMEM)


def vmem():
    return pl.BlockSpec(memory_space=pltpu.VMEM)


def per_device(
    left_env,
    site_tensor,
    right_env,
    center,
    mpo_table,
    update_terms,
    update_count,
    heff_terms,
    heff_count,
):
    chain, mine = lax.axis_size("chain"), lax.axis_index("chain")
    place = mine.reshape(1).astype(jnp.int32)
    blocks, rows, cols = left_env.shape
    slots = heff_terms.shape[0]
    update_terms, heff_terms = update_terms.T, heff_terms.T
    params = pltpu.CompilerParams(vmem_limit_bytes=VMEM_LIMIT)
    tile = jax.ShapeDtypeStruct(TILE, jnp.float32)

    fresh, squares = pl.pallas_call(
        update_kernel,
        out_shape=(jax.ShapeDtypeStruct(left_env.shape, jnp.bfloat16), tile),
        in_specs=[smem(), smem(), smem(), smem(), vmem(), vmem()],
        out_specs=(vmem(), vmem()),
        scratch_shapes=[
            pltpu.VMEM((blocks, cols, rows), jnp.bfloat16),
            pltpu.VMEM((update_terms.shape[1], cols, cols), jnp.bfloat16),
            pltpu.VMEM((blocks, cols, cols), jnp.float32),
        ],
        compiler_params=params,
        cost_estimate=pl.CostEstimate(flops=10**9, bytes_accessed=6 * 2**20, transcendentals=0),
        name="update",
    )(place, update_count, update_terms, mpo_table, left_env, site_tensor)

    incoming = lax.ppermute(fresh, "chain", [(k, k + 1) for k in range(chain - 1)])

    def current(step, count, *rest):
        return (jnp.minimum(step, (count[0] - 1) // GROUP), 0, 0)

    half, passed = pl.pallas_call(
        half_kernel,
        out_shape=(jax.ShapeDtypeStruct((slots,) + center.shape[1:], jnp.bfloat16), tile),
        grid_spec=pltpu.PrefetchScalarGridSpec(
            num_scalar_prefetch=2,
            grid=(slots // GROUP,),
            in_specs=[smem(), vmem(), vmem(), vmem()],
            out_specs=(pl.BlockSpec((GROUP, rows, cols), current), vmem()),
        ),
        compiler_params=params,
        cost_estimate=pl.CostEstimate(flops=10**9, bytes_accessed=8 * 2**20, transcendentals=0),
        name="half",
    )(heff_count, heff_terms, mpo_table, center, right_env, squares)

    number = jax.ShapeDtypeStruct((1,), jnp.float32)
    log_scale, scale = pl.pallas_call(
        lambda *refs: exchange_kernel(float(left_env.size), *refs),
        out_shape=(number, number),
        in_specs=[vmem()],
        out_specs=(smem(), smem()),
        scratch_shapes=[
            pltpu.VMEM((chain,) + TILE, jnp.float32),
            pltpu.SemaphoreType.DMA((chain,)),
            pltpu.SemaphoreType.DMA((chain,)),
        ],
        compiler_params=pltpu.CompilerParams(collective_id=0, has_side_effects=True),
        cost_estimate=pl.CostEstimate(flops=10**5, bytes_accessed=2**20, transcendentals=0),
        name="exchange",
    )(passed)

    product = pl.pallas_call(
        product_kernel,
        out_shape=jax.ShapeDtypeStruct(center.shape, jnp.bfloat16),
        grid_spec=pltpu.PrefetchScalarGridSpec(
            num_scalar_prefetch=2,
            grid=(slots // GROUP,),
            in_specs=[
                smem(),
                smem(),
                pl.BlockSpec((GROUP, rows, cols), current),
                pl.BlockSpec(memory_space=pl.ANY),
                pl.BlockSpec(memory_space=pl.ANY),
            ],
            out_specs=vmem(),
            scratch_shapes=[
                pltpu.VMEM(left_env.shape, jnp.bfloat16),
                pltpu.VMEM(center.shape, jnp.float32),
                pltpu.SemaphoreType.DMA,
            ],
        ),
        compiler_params=params,
        name="product",
    )(heff_count, heff_terms, place, scale, half, left_env, incoming)
    return (product, log_scale)


def solution(mesh):
    placed = (
        P(("grp", "chain"), None, None),
        P(("grp", "chain"), None, None),
        P(("grp", "chain"), None, None),
        P(("grp", "chain"), None, None),
        P(),
        P(("grp", "chain"), None),
        P(("grp", "chain")),
        P(("grp", "chain"), None),
        P(("grp", "chain")),
    )
    return jax.shard_map(
        per_device,
        mesh=mesh,
        in_specs=placed,
        out_specs=(P(("grp", "chain"), None, None), P(("grp", "chain"))),
        check_vma=False,
    )
```

```python
import functools

import jax
import jax.numpy as jnp
from jax import lax
from jax.experimental import pallas as pl
from jax.experimental.pallas import tpu as pltpu
from jax.sharding import PartitionSpec as P

UNROLL = 8
VMEM_LIMIT = 32 * 1024 * 1024
TILE = (8, 128)


def dot(a, b):
    return jnp.dot(a, b, preferred_element_type=jnp.float32)


def sort_slots(count, keys, border, order, sizes):
    stride = order.shape[0] // 2
    live = count[0]

    def advance(g, carry):
        low, high = carry
        for u in range(UNROLL):
            t = g * UNROLL + u
            upper = (keys(t) >= border).astype(jnp.int32)
            order[jnp.where(upper == 1, stride + high, low)] = t
            valid = (t < live).astype(jnp.int32)
            low, high = low + valid * (1 - upper), high + valid * upper
        return low, high

    zero = jnp.int32(0)
    low, high = lax.fori_loop(0, (live + UNROLL - 1) // UNROLL, advance, (zero, zero))
    for u in range(UNROLL):
        order[low + u] = 0
        order[stride + high + u] = 0
    sizes[0] = low
    sizes[1] = high


def update_list(index, order, sizes, terms, table, left, site, site_t, fresh, parts, acc):
    chunk = acc.shape[0]
    base = index * (order.shape[0] // 2)
    live = sizes[index]
    groups = (live + UNROLL - 1) // UNROLL

    def clear(k, carry):
        acc[k] = jnp.zeros(acc.shape[1:], jnp.float32)
        return carry

    lax.fori_loop(0, chunk, clear, 0, unroll=4)

    def first(g, carry):
        for u in range(UNROLL):
            s = g * UNROLL + u
            t = order[base + s]
            coef = jnp.where(s < live, table[terms[4, t]], 0.0)
            part = dot(site_t[terms[1, t]], left[terms[0, t]]) * coef
            parts[s] = part.astype(jnp.bfloat16)
        return carry

    lax.fori_loop(0, groups, first, 0)

    def second(g, carry):
        sums = []
        for u in range(UNROLL):
            s = g * UNROLL + u
            t = order[base + s]
            o = terms[3, t]
            o = jnp.where(o >= chunk, o - chunk, o)
            sums.append((o, dot(parts[s], site[terms[2, t]])))
        for o, full in sums:
            acc[o] += full
        return carry

    lax.fori_loop(0, groups, second, 0)

    def finish(k, total):
        rounded = acc[k].astype(jnp.bfloat16)
        fresh[k] = rounded.T
        wide = rounded.astype(jnp.float32)
        return total + wide * wide

    zero = jnp.zeros(acc.shape[1:], jnp.float32)
    return jnp.sum(lax.fori_loop(0, chunk, finish, zero, unroll=4))


def update_low_kernel(
    place, count, terms, table, left, site, fresh, squares, site_t, order, sizes, parts, acc
):
    blocks = left.shape[0]
    sort_slots(count, lambda t: terms[3, t], acc.shape[0], order, sizes)

    def prepare(k, carry):
        site_t[k] = site[k].T
        return carry

    lax.fori_loop(0, blocks, prepare, 0, unroll=4)
    total = update_list(0, order, sizes, terms, table, left, site, site_t, fresh, parts, acc)
    squares[...] = jnp.full(TILE, total)

    @pl.when(place[0] == 0)
    def _():
        def add(k, total):
            wide = left[k].astype(jnp.float32)
            return total + wide * wide

        zero = jnp.zeros(acc.shape[1:], jnp.float32)
        total = lax.fori_loop(0, blocks, add, zero, unroll=4)
        squares[1:, :] = jnp.full((TILE[0] - 1, TILE[1]), jnp.sum(total))


def update_high_kernel(
    order, sizes, terms, table, left, site, site_t, earlier, fresh, squares, parts, acc
):
    total = update_list(1, order, sizes, terms, table, left, site, site_t, fresh, parts, acc)
    squares[...] = earlier[...]
    squares[0:1, :] = earlier[0:1, :] + jnp.full((1, TILE[1]), total)


def half_kernel(count, terms, table, center, right, half, order, sizes, border):
    sort_slots(count, lambda t: terms[0, t], border, order, sizes)

    def advance(g, carry):
        for u in range(UNROLL):
            t = g * UNROLL + u
            coef = jnp.where(t < count[0], table[terms[4, t]] * table[terms[5, t]], 0.0)
            value = dot(center[terms[1, t]], right[terms[2, t]]) * coef
            half[t] = value.astype(jnp.bfloat16)
        return carry

    lax.fori_loop(0, (count[0] + UNROLL - 1) // UNROLL, advance, 0)


def exchange_kernel(size, squares, log_scale, scale, held, send_sem, recv_sem):
    chain, mine = held.shape[0], lax.axis_index("chain")
    held[...] = jnp.zeros(held.shape, jnp.float32)
    held[mine] = squares[...]
    barrier = pltpu.get_barrier_semaphore()

    def copy(source, target):
        return pltpu.make_async_remote_copy(
            src_ref=squares,
            dst_ref=held.at[source],
            send_sem=send_sem.at[target],
            recv_sem=recv_sem.at[source],
            device_id={"chain": target},
            device_id_type=pl.DeviceIdType.MESH,
        )

    def greet(k, carry):
        @pl.when(k != mine)
        def _():
            pl.semaphore_signal(
                barrier, inc=1, device_id={"chain": k}, device_id_type=pl.DeviceIdType.MESH
            )

        return carry

    lax.fori_loop(0, chain, greet, 0)
    pl.semaphore_wait(barrier, chain - 1)

    def send(k, carry):
        copy(mine, k).start()
        return carry

    def sent(k, carry):
        copy(mine, k).wait_send()
        return carry

    def arrived(k, carry):
        copy(k, mine).wait_recv()
        return carry

    lax.fori_loop(mine + 1, chain, send, 0)
    lax.fori_loop(0, mine, arrived, 0)
    lax.fori_loop(mine + 1, chain, sent, 0)
    scales = jnp.sqrt(held[...] / size + 1e-06)
    logs = jnp.log(scales)
    segment = lax.broadcasted_iota(jnp.int32, held.shape, 0)
    row = lax.broadcasted_iota(jnp.int32, held.shape, 1)
    lane = lax.broadcasted_iota(jnp.int32, held.shape, 2)
    opening = (segment == 0) & (row == 1)
    passed = (segment < mine) & (row == 0)
    log_scale[0] = jnp.sum(jnp.where((opening | passed) & (lane == 0), logs, 0.0))
    behind = (segment == jnp.maximum(mine - 1, 0)) & (row == jnp.where(mine == 0, 1, 0))
    scale[0] = jnp.sum(jnp.where(behind & (lane == 0), scales, 0.0))


def product_list(index, place, order, sizes, terms, half, left, seam, acc):
    chunk = seam.shape[0]
    base = index * (order.shape[0] // 2)
    live = sizes[index]
    groups = (live + UNROLL - 1) // UNROLL

    def advance(opening, g, carry):
        sums = []
        for u in range(UNROLL):
            s = g * UNROLL + u
            t = order[base + s]
            e = terms[0, t]
            e = jnp.where(e >= chunk, e - chunk, e)
            block = left[index * chunk + e].T if opening else seam[e]
            valid = jnp.full((1, acc.shape[2]), s) < live
            sums.append((terms[3, t], jnp.where(valid, dot(block, half[t]), 0.0)))
        for o, full in sums:
            acc[o] += full
        return carry

    for opening in (False, True):

        @pl.when((place[0] == 0) == opening)
        def _():
            lax.fori_loop(0, groups, functools.partial(advance, opening), 0)


def product_low_kernel(place, order, sizes, terms, half, left, seam, squares, acc, passed):
    passed[...] = squares[...]

    def clear(k, carry):
        acc[k] = jnp.zeros(acc.shape[1:], jnp.float32)
        return carry

    lax.fori_loop(0, acc.shape[0], clear, 0, unroll=4)
    product_list(0, place, order, sizes, terms, half, left, seam, acc)


def product_high_kernel(place, order, sizes, terms, scale, half, left, seam, acc_in, product, acc):
    def load(k, carry):
        acc[k] = acc_in[k]
        return carry

    lax.fori_loop(0, acc.shape[0], load, 0, unroll=4)
    product_list(1, place, order, sizes, terms, half, left, seam, acc)
    inverse = 1.0 / jnp.full((1, acc.shape[2]), scale[0])

    def finish(k, carry):
        product[k] = (acc[k] * inverse).astype(jnp.bfloat16)
        return carry

    lax.fori_loop(0, acc.shape[0], finish, 0, unroll=4)


def smem():
    return pl.BlockSpec(memory_space=pltpu.SMEM)


def vmem():
    return pl.BlockSpec(memory_space=pltpu.VMEM)


def per_device(
    left_env,
    site_tensor,
    right_env,
    center,
    mpo_table,
    update_terms,
    update_count,
    heff_terms,
    heff_count,
):
    chain, mine = lax.axis_size("chain"), lax.axis_index("chain")
    place = mine.reshape(1).astype(jnp.int32)
    blocks, rows, cols = left_env.shape
    chunk = blocks // 2
    update_terms, heff_terms = update_terms.T, heff_terms.T
    params = pltpu.CompilerParams(vmem_limit_bytes=VMEM_LIMIT)

    def shaped(shape, dtype):
        return jax.ShapeDtypeStruct(shape, dtype)

    def cost(microseconds):
        return pl.CostEstimate(
            flops=int(microseconds * 10**9), bytes_accessed=2**20, transcendentals=0
        )

    tile = shaped(TILE, jnp.float32)
    turned = shaped((blocks, cols, rows), jnp.bfloat16)
    piece = shaped((chunk, rows, cols), jnp.bfloat16)
    sums = shaped(center.shape, jnp.float32)
    two = shaped((2,), jnp.int32)

    def listed(terms):
        return shaped((2 * (terms.shape[1] + UNROLL),), jnp.int32)

    working = [
        pltpu.VMEM((update_terms.shape[1], cols, cols), jnp.bfloat16),
        pltpu.VMEM((chunk, cols, cols), jnp.float32),
    ]
    low, squares, site_t, order, sizes = pl.pallas_call(
        update_low_kernel,
        out_shape=(piece, tile, turned, listed(update_terms), two),
        in_specs=[smem(), smem(), smem(), smem(), vmem(), vmem()],
        out_specs=(vmem(), vmem(), vmem(), smem(), smem()),
        scratch_shapes=working,
        compiler_params=params,
        cost_estimate=cost(9),
        name="update_low",
    )(place, update_count, update_terms, mpo_table, left_env, site_tensor)
    pairs = [(k, k + 1) for k in range(chain - 1)]
    seam_low = lax.ppermute(low, "chain", pairs)

    high, squares = pl.pallas_call(
        update_high_kernel,
        out_shape=(piece, tile),
        in_specs=[smem(), smem(), smem(), smem(), vmem(), vmem(), vmem(), vmem()],
        out_specs=(vmem(), vmem()),
        scratch_shapes=working,
        compiler_params=params,
        cost_estimate=cost(5),
        name="update_high",
    )(order, sizes, update_terms, mpo_table, left_env, site_tensor, site_t, squares)
    seam_high = lax.ppermute(high, "chain", pairs)

    half, order, sizes = pl.pallas_call(
        functools.partial(half_kernel, border=chunk),
        out_shape=(
            shaped((heff_terms.shape[1],) + center.shape[1:], jnp.bfloat16),
            listed(heff_terms),
            two,
        ),
        in_specs=[smem(), smem(), smem(), vmem(), vmem()],
        out_specs=(vmem(), smem(), smem()),
        compiler_params=params,
        cost_estimate=cost(5),
        name="half",
    )(heff_count, heff_terms, mpo_table, center, right_env)

    acc, passed = pl.pallas_call(
        product_low_kernel,
        out_shape=(sums, tile),
        in_specs=[smem(), smem(), smem(), smem(), vmem(), vmem(), vmem(), vmem()],
        out_specs=(vmem(), vmem()),
        compiler_params=params,
        cost_estimate=cost(4),
        name="product_low",
    )(place, order, sizes, heff_terms, half, left_env, seam_low, squares)

    number = shaped((1,), jnp.float32)
    log_scale, scale = pl.pallas_call(
        lambda *refs: exchange_kernel(float(left_env.size), *refs),
        out_shape=(number, number),
        in_specs=[vmem()],
        out_specs=(smem(), smem()),
        scratch_shapes=[
            pltpu.VMEM((chain,) + TILE, jnp.float32),
            pltpu.SemaphoreType.DMA((chain,)),
            pltpu.SemaphoreType.DMA((chain,)),
        ],
        compiler_params=pltpu.CompilerParams(collective_id=0, has_side_effects=True),
        cost_estimate=cost(3),
        name="exchange",
    )(passed)

    product = pl.pallas_call(
        product_high_kernel,
        out_shape=shaped(center.shape, jnp.bfloat16),
        in_specs=[smem(), smem(), smem(), smem(), smem(), vmem(), vmem(), vmem(), vmem()],
        out_specs=vmem(),
        scratch_shapes=[pltpu.VMEM(center.shape, jnp.float32)],
        compiler_params=params,
        cost_estimate=cost(6),
        name="product_high",
    )(place, order, sizes, heff_terms, scale, half, left_env, seam_high, acc)
    return (product, log_scale)


def solution(mesh):
    placed = (
        P(("grp", "chain"), None, None),
        P(("grp", "chain"), None, None),
        P(("grp", "chain"), None, None),
        P(("grp", "chain"), None, None),
        P(),
        P(("grp", "chain"), None),
        P(("grp", "chain")),
        P(("grp", "chain"), None),
        P(("grp", "chain")),
    )
    return jax.shard_map(
        per_device,
        mesh=mesh,
        in_specs=placed,
        out_specs=(P(("grp", "chain"), None, None), P(("grp", "chain"))),
        check_vma=False,
    )
```

```python
import functools

import jax
import jax.numpy as jnp
from jax import lax
from jax.experimental import pallas as pl
from jax.experimental.pallas import tpu as pltpu
from jax.sharding import PartitionSpec as P

UNROLL = 16
VMEM_LIMIT = 32 * 1024 * 1024
TILE = (1, 128)


def dot(a, b):
    return jnp.dot(a, b, preferred_element_type=jnp.float32)


def sort_slots(count, keys, border, order, sizes, coefs=None, coef=None):
    stride = order.shape[0] // 2
    live = count[0]

    def advance(g, carry):
        low, high = carry
        for u in range(UNROLL):
            t = g * UNROLL + u
            upper = (keys(t) >= border).astype(jnp.int32)
            place = jnp.where(upper == 1, stride + high, low)
            order[place] = t
            if coefs is not None:
                coefs[place] = coef(t)
            valid = (t < live).astype(jnp.int32)
            low, high = low + valid * (1 - upper), high + valid * upper
        return low, high

    zero = jnp.int32(0)
    low, high = lax.fori_loop(0, (live + UNROLL - 1) // UNROLL, advance, (zero, zero))
    for u in range(UNROLL):
        order[low + u] = 0
        order[stride + high + u] = 0
    sizes[0] = low
    sizes[1] = high


def update_list(index, order, sizes, coefs, terms, left, site, site_t, fresh, parts, acc):
    chunk = acc.shape[0]
    base = index * (order.shape[0] // 2)
    live = sizes[index]
    groups = (live + UNROLL - 1) // UNROLL

    def clear(k, carry):
        acc[k] = jnp.zeros(acc.shape[1:], jnp.float32)
        return carry

    lax.fori_loop(0, chunk, clear, 0, unroll=4)

    def first(g, carry):
        for u in range(UNROLL):
            s = g * UNROLL + u
            t = order[base + s]
            coef = jnp.where(s < live, coefs[base + s], 0.0)
            part = dot(site_t[terms[1, t]], left[terms[0, t]]) * coef
            parts[s] = part.astype(jnp.bfloat16)
        return carry

    lax.fori_loop(0, groups, first, 0)

    def second(g, carry):
        sums = []
        for u in range(UNROLL):
            s = g * UNROLL + u
            t = order[base + s]
            o = terms[3, t]
            o = jnp.where(o >= chunk, o - chunk, o)
            sums.append((o, dot(parts[s], site[terms[2, t]])))
        for o, full in sums:
            acc[o] += full
        return carry

    lax.fori_loop(0, groups, second, 0)

    def finish(k, total):
        rounded = acc[k].astype(jnp.bfloat16)
        fresh[k] = rounded.T
        wide = rounded.astype(jnp.float32)
        return total + wide * wide

    zero = jnp.zeros(acc.shape[1:], jnp.float32)
    return jnp.sum(lax.fori_loop(0, chunk, finish, zero, unroll=4))


def list_kernel(count, terms, table, order, sizes, coefs, border):
    sort_slots(
        count, lambda t: terms[3, t], border, order, sizes, coefs, lambda t: table[terms[4, t]]
    )


def update_low_kernel(
    place, order, sizes, coefs, terms, left, site, fresh, squares, site_t, parts, acc
):
    blocks = left.shape[0]

    def prepare(k, carry):
        site_t[k] = site[k].T
        return carry

    lax.fori_loop(0, blocks, prepare, 0, unroll=4)
    total = update_list(0, order, sizes, coefs, terms, left, site, site_t, fresh, parts, acc)
    lane = lax.broadcasted_iota(jnp.int32, TILE, 1)
    squares[...] = jnp.where(lane == 0, total, 0.0)

    @pl.when(place[0] == 0)
    def _():
        def add(k, total):
            wide = left[k].astype(jnp.float32)
            return total + wide * wide

        zero = jnp.zeros(acc.shape[1:], jnp.float32)
        opening = jnp.sum(lax.fori_loop(0, blocks, add, zero, unroll=4))
        squares[...] = jnp.where(lane == 1, opening, squares[...])


def update_high_kernel(
    order, sizes, coefs, terms, left, site, site_t, earlier, fresh, squares, parts, acc
):
    total = update_list(1, order, sizes, coefs, terms, left, site, site_t, fresh, parts, acc)
    lane = lax.broadcasted_iota(jnp.int32, TILE, 1)
    squares[...] = earlier[...] + jnp.where(lane == 0, total, 0.0)


def half_kernel(count, terms, table, center, right, half, order, sizes, border):
    sort_slots(count, lambda t: terms[0, t], border, order, sizes)

    def advance(g, carry):
        for u in range(UNROLL):
            t = g * UNROLL + u
            coef = jnp.where(t < count[0], table[terms[4, t]] * table[terms[5, t]], 0.0)
            value = dot(center[terms[1, t]], right[terms[2, t]]) * coef
            half[t] = value.astype(jnp.bfloat16)
        return carry

    lax.fori_loop(0, (count[0] + UNROLL - 1) // UNROLL, advance, 0)


def exchange_kernel(size, squares, log_scale, scale, held, send_sem, recv_sem):
    chain, mine = held.shape[0], lax.axis_index("chain")
    held[...] = jnp.zeros(held.shape, jnp.float32)
    held[mine] = squares[...]
    barrier = pltpu.get_barrier_semaphore()

    def copy(source, target):
        return pltpu.make_async_remote_copy(
            src_ref=squares,
            dst_ref=held.at[source],
            send_sem=send_sem.at[target],
            recv_sem=recv_sem.at[source],
            device_id={"chain": target},
            device_id_type=pl.DeviceIdType.MESH,
        )

    def greet(k, carry):
        @pl.when(k != mine)
        def _():
            pl.semaphore_signal(
                barrier, inc=1, device_id={"chain": k}, device_id_type=pl.DeviceIdType.MESH
            )

        return carry

    lax.fori_loop(0, chain, greet, 0)
    pl.semaphore_wait(barrier, chain - 1)

    def send(k, carry):
        copy(mine, k).start()
        return carry

    def sent(k, carry):
        copy(mine, k).wait_send()
        return carry

    def arrived(k, carry):
        copy(k, mine).wait_recv()
        return carry

    lax.fori_loop(mine + 1, chain, send, 0)
    lax.fori_loop(0, mine, arrived, 0)
    lax.fori_loop(mine + 1, chain, sent, 0)
    scales = jnp.sqrt(held[...] / size + 1e-06)
    logs = jnp.log(scales)
    segment = lax.broadcasted_iota(jnp.int32, held.shape, 0)
    lane = lax.broadcasted_iota(jnp.int32, held.shape, 2)
    opening = (segment == 0) & (lane == 1)
    passed = (segment < mine) & (lane == 0)
    log_scale[0] = jnp.sum(jnp.where(opening | passed, logs, 0.0))
    behind = (segment == jnp.maximum(mine - 1, 0)) & (lane == jnp.where(mine == 0, 1, 0))
    scale[0] = jnp.sum(jnp.where(behind, scales, 0.0))


def product_list(index, place, order, sizes, terms, half, left, seam, acc):
    chunk = seam.shape[0]
    base = index * (order.shape[0] // 2)
    live = sizes[index]
    groups = (live + UNROLL - 1) // UNROLL

    def advance(opening, g, carry):
        sums = []
        for u in range(UNROLL):
            s = g * UNROLL + u
            t = order[base + s]
            e = terms[0, t]
            e = jnp.where(e >= chunk, e - chunk, e)
            block = left[index * chunk + e].T if opening else seam[e]
            valid = jnp.full((1, acc.shape[2]), s) < live
            sums.append((terms[3, t], jnp.where(valid, dot(block, half[t]), 0.0)))
        for o, full in sums:
            acc[o] += full
        return carry

    for opening in (False, True):

        @pl.when((place[0] == 0) == opening)
        def _():
            lax.fori_loop(0, groups, functools.partial(advance, opening), 0)


def product_low_kernel(place, order, sizes, terms, half, left, seam, squares, acc, passed):
    passed[...] = squares[...]

    def clear(k, carry):
        acc[k] = jnp.zeros(acc.shape[1:], jnp.float32)
        return carry

    lax.fori_loop(0, acc.shape[0], clear, 0, unroll=4)
    product_list(0, place, order, sizes, terms, half, left, seam, acc)


def product_high_kernel(place, order, sizes, terms, scale, half, left, seam, acc_in, product, acc):
    def load(k, carry):
        acc[k] = acc_in[k]
        return carry

    lax.fori_loop(0, acc.shape[0], load, 0, unroll=4)
    product_list(1, place, order, sizes, terms, half, left, seam, acc)
    inverse = 1.0 / jnp.full((1, acc.shape[2]), scale[0])

    def finish(k, carry):
        product[k] = (acc[k] * inverse).astype(jnp.bfloat16)
        return carry

    lax.fori_loop(0, acc.shape[0], finish, 0, unroll=4)


def smem():
    return pl.BlockSpec(memory_space=pltpu.SMEM)


def vmem():
    return pl.BlockSpec(memory_space=pltpu.VMEM)


def per_device(
    left_env,
    site_tensor,
    right_env,
    center,
    mpo_table,
    update_terms,
    update_count,
    heff_terms,
    heff_count,
):
    chain, mine = lax.axis_size("chain"), lax.axis_index("chain")
    place = mine.reshape(1).astype(jnp.int32)
    blocks, rows, cols = left_env.shape
    chunk = blocks // 2
    update_terms, heff_terms = update_terms.T, heff_terms.T
    params = pltpu.CompilerParams(vmem_limit_bytes=VMEM_LIMIT)

    def shaped(shape, dtype):
        return jax.ShapeDtypeStruct(shape, dtype)

    def cost(microseconds):
        return pl.CostEstimate(
            flops=int(microseconds * 10**9), bytes_accessed=2**20, transcendentals=0
        )

    tile = shaped(TILE, jnp.float32)
    turned = shaped((blocks, cols, rows), jnp.bfloat16)
    piece = shaped((chunk, rows, cols), jnp.bfloat16)
    sums = shaped(center.shape, jnp.float32)
    two = shaped((2,), jnp.int32)

    def listed(terms, dtype=jnp.int32):
        return shaped((2 * (terms.shape[1] + UNROLL),), dtype)

    working = [
        pltpu.VMEM((update_terms.shape[1], cols, cols), jnp.bfloat16),
        pltpu.VMEM((chunk, cols, cols), jnp.float32),
    ]
    order, sizes, coefs = pl.pallas_call(
        functools.partial(list_kernel, border=chunk),
        out_shape=(listed(update_terms), two, listed(update_terms, jnp.float32)),
        in_specs=[smem(), smem(), smem()],
        out_specs=(smem(), smem(), smem()),
        compiler_params=params,
        cost_estimate=cost(4),
        name="list_slots",
    )(update_count, update_terms, mpo_table)

    low, squares, site_t = pl.pallas_call(
        update_low_kernel,
        out_shape=(piece, tile, turned),
        in_specs=[smem(), smem(), smem(), smem(), smem(), vmem(), vmem()],
        out_specs=(vmem(), vmem(), vmem()),
        scratch_shapes=working,
        compiler_params=params,
        cost_estimate=cost(9),
        name="update_low",
    )(place, order, sizes, coefs, update_terms, left_env, site_tensor)
    pairs = [(k, k + 1) for k in range(chain - 1)]
    seam_low = lax.ppermute(low, "chain", pairs)

    high, squares = pl.pallas_call(
        update_high_kernel,
        out_shape=(piece, tile),
        in_specs=[smem(), smem(), smem(), smem(), vmem(), vmem(), vmem(), vmem()],
        out_specs=(vmem(), vmem()),
        scratch_shapes=working,
        compiler_params=params,
        cost_estimate=cost(5),
        name="update_high",
    )(order, sizes, coefs, update_terms, left_env, site_tensor, site_t, squares)
    seam_high = lax.ppermute(high, "chain", pairs)

    half, order, sizes = pl.pallas_call(
        functools.partial(half_kernel, border=chunk),
        out_shape=(
            shaped((heff_terms.shape[1],) + center.shape[1:], jnp.bfloat16),
            listed(heff_terms),
            two,
        ),
        in_specs=[smem(), smem(), smem(), vmem(), vmem()],
        out_specs=(vmem(), smem(), smem()),
        compiler_params=params,
        cost_estimate=cost(5),
        name="half",
    )(heff_count, heff_terms, mpo_table, center, right_env)

    acc, passed = pl.pallas_call(
        product_low_kernel,
        out_shape=(sums, tile),
        in_specs=[smem(), smem(), smem(), smem(), vmem(), vmem(), vmem(), vmem()],
        out_specs=(vmem(), vmem()),
        compiler_params=params,
        cost_estimate=cost(4),
        name="product_low",
    )(place, order, sizes, heff_terms, half, left_env, seam_low, squares)

    number = shaped((1,), jnp.float32)
    log_scale, scale = pl.pallas_call(
        lambda *refs: exchange_kernel(float(left_env.size), *refs),
        out_shape=(number, number),
        in_specs=[vmem()],
        out_specs=(smem(), smem()),
        scratch_shapes=[
            pltpu.VMEM((chain,) + TILE, jnp.float32),
            pltpu.SemaphoreType.DMA((chain,)),
            pltpu.SemaphoreType.DMA((chain,)),
        ],
        compiler_params=pltpu.CompilerParams(
            collective_id=0, has_side_effects=True, vmem_limit_bytes=4 * 1024 * 1024
        ),
        cost_estimate=cost(3),
        name="exchange",
    )(passed)

    product = pl.pallas_call(
        product_high_kernel,
        out_shape=shaped(center.shape, jnp.bfloat16),
        in_specs=[smem(), smem(), smem(), smem(), smem(), vmem(), vmem(), vmem(), vmem()],
        out_specs=vmem(),
        scratch_shapes=[pltpu.VMEM(center.shape, jnp.float32)],
        compiler_params=params,
        cost_estimate=cost(6),
        name="product_high",
    )(place, order, sizes, heff_terms, scale, half, left_env, seam_high, acc)
    return (product, log_scale)


def solution(mesh):
    placed = (
        P(("grp", "chain"), None, None),
        P(("grp", "chain"), None, None),
        P(("grp", "chain"), None, None),
        P(("grp", "chain"), None, None),
        P(),
        P(("grp", "chain"), None),
        P(("grp", "chain")),
        P(("grp", "chain"), None),
        P(("grp", "chain")),
    )
    return jax.shard_map(
        per_device,
        mesh=mesh,
        in_specs=placed,
        out_specs=(P(("grp", "chain"), None, None), P(("grp", "chain"))),
        check_vma=False,
    )
```

```python
import functools

import jax
import jax.numpy as jnp
from jax import lax
from jax.experimental import pallas as pl
from jax.experimental.pallas import tpu as pltpu
from jax.sharding import PartitionSpec as P

UNROLL = 16
VMEM_LIMIT = 32 * 1024 * 1024
TILE = (1, 128)


def dot(a, b):
    return jnp.dot(a, b, preferred_element_type=jnp.float32)


def sort_slots(count, keys, borders, order, sizes, coefs=None, coef=None):
    lists = len(borders) - 1
    stride = order.shape[0] // lists
    live = count[0]

    def advance(g, lengths):
        for u in range(UNROLL):
            t = g * UNROLL + u
            key = keys(t)
            inside = [
                ((key >= borders[i]) & (key < borders[i + 1])).astype(jnp.int32)
                for i in range(lists)
            ]
            place = sum(inside[i] * (i * stride + lengths[i]) for i in range(lists))
            order[place] = t
            if coefs is not None:
                coefs[place] = coef(t)
            valid = (t < live).astype(jnp.int32)
            lengths = tuple(lengths[i] + inside[i] * valid for i in range(lists))
        return lengths

    lengths = lax.fori_loop(
        0, (live + UNROLL - 1) // UNROLL, advance, (jnp.int32(0),) * lists
    )
    for i in range(lists):
        for u in range(UNROLL):
            order[i * stride + lengths[i] + u] = 0
        sizes[i] = lengths[i]


def update_list(index, borders, order, sizes, coefs, terms, left, site, site_t, fresh, parts, acc):
    chunk = acc.shape[0]
    base = index * (order.shape[0] // (len(borders) - 1))
    live = sizes[index]
    groups = (live + UNROLL - 1) // UNROLL

    def clear(k, carry):
        acc[k] = jnp.zeros(acc.shape[1:], jnp.float32)
        return carry

    lax.fori_loop(0, chunk, clear, 0, unroll=4)

    def first(g, carry):
        for u in range(UNROLL):
            s = g * UNROLL + u
            t = order[base + s]
            coef = jnp.where(s < live, coefs[base + s], 0.0)
            part = dot(site_t[terms[1, t]], left[terms[0, t]]) * coef
            parts[s] = part.astype(jnp.bfloat16)
        return carry

    lax.fori_loop(0, groups, first, 0)

    def second(g, carry):
        sums = []
        for u in range(UNROLL):
            s = g * UNROLL + u
            t = order[base + s]
            o = jnp.clip(terms[3, t] - borders[index], 0, chunk - 1)
            sums.append((o, dot(parts[s], site[terms[2, t]])))
        for o, full in sums:
            acc[o] += full
        return carry

    lax.fori_loop(0, groups, second, 0)

    def finish(k, total):
        rounded = acc[k].astype(jnp.bfloat16)
        fresh[k] = rounded.T
        wide = rounded.astype(jnp.float32)
        return total + wide * wide

    zero = jnp.zeros(acc.shape[1:], jnp.float32)
    return jnp.sum(lax.fori_loop(0, chunk, finish, zero, unroll=4))


def list_kernel(count, terms, table, order, sizes, coefs, borders):
    sort_slots(
        count, lambda t: terms[3, t], borders, order, sizes, coefs, lambda t: table[terms[4, t]]
    )


def update_first_kernel(
    place, order, sizes, coefs, terms, left, site, fresh, squares, site_t, parts, acc, borders
):
    blocks = left.shape[0]

    def prepare(k, carry):
        site_t[k] = site[k].T
        return carry

    lax.fori_loop(0, blocks, prepare, 0, unroll=4)
    total = update_list(0, borders, order, sizes, coefs, terms, left, site, site_t, fresh, parts, acc)
    lane = lax.broadcasted_iota(jnp.int32, TILE, 1)
    squares[...] = jnp.where(lane == 0, total, 0.0)

    @pl.when(place[0] == 0)
    def _():
        def add(k, total):
            wide = left[k].astype(jnp.float32)
            return total + wide * wide

        zero = jnp.zeros(acc.shape[1:], jnp.float32)
        opening = jnp.sum(lax.fori_loop(0, blocks, add, zero, unroll=4))
        squares[...] = jnp.where(lane == 1, opening, squares[...])


def update_next_kernel(
    order, sizes, coefs, terms, left, site, site_t, earlier, fresh, squares, parts, acc,
    index, borders,
):
    total = update_list(
        index, borders, order, sizes, coefs, terms, left, site, site_t, fresh, parts, acc
    )
    lane = lax.broadcasted_iota(jnp.int32, TILE, 1)
    squares[...] = earlier[...] + jnp.where(lane == 0, total, 0.0)


def half_kernel(count, terms, table, center, right, half, order, sizes, borders):
    sort_slots(count, lambda t: terms[0, t], borders, order, sizes)

    def advance(g, carry):
        for u in range(UNROLL):
            t = g * UNROLL + u
            coef = jnp.where(t < count[0], table[terms[4, t]] * table[terms[5, t]], 0.0)
            value = dot(center[terms[1, t]], right[terms[2, t]]) * coef
            half[t] = value.astype(jnp.bfloat16)
        return carry

    lax.fori_loop(0, (count[0] + UNROLL - 1) // UNROLL, advance, 0)


def exchange_kernel(size, squares, log_scale, scale, held, send_sem, recv_sem):
    chain, mine = held.shape[0], lax.axis_index("chain")
    held[...] = jnp.zeros(held.shape, jnp.float32)
    held[mine] = squares[...]
    barrier = pltpu.get_barrier_semaphore()

    def copy(source, target):
        return pltpu.make_async_remote_copy(
            src_ref=squares,
            dst_ref=held.at[source],
            send_sem=send_sem.at[target],
            recv_sem=recv_sem.at[source],
            device_id={"chain": target},
            device_id_type=pl.DeviceIdType.MESH,
        )

    def greet(k, carry):
        @pl.when(k != mine)
        def _():
            pl.semaphore_signal(
                barrier, inc=1, device_id={"chain": k}, device_id_type=pl.DeviceIdType.MESH
            )

        return carry

    lax.fori_loop(0, chain, greet, 0)
    pl.semaphore_wait(barrier, chain - 1)

    def send(k, carry):
        copy(mine, k).start()
        return carry

    def sent(k, carry):
        copy(mine, k).wait_send()
        return carry

    def arrived(k, carry):
        copy(k, mine).wait_recv()
        return carry

    lax.fori_loop(mine + 1, chain, send, 0)
    lax.fori_loop(0, mine, arrived, 0)
    lax.fori_loop(mine + 1, chain, sent, 0)
    scales = jnp.sqrt(held[...] / size + 1e-06)
    logs = jnp.log(scales)
    segment = lax.broadcasted_iota(jnp.int32, held.shape, 0)
    lane = lax.broadcasted_iota(jnp.int32, held.shape, 2)
    opening = (segment == 0) & (lane == 1)
    passed = (segment < mine) & (lane == 0)
    log_scale[0] = jnp.sum(jnp.where(opening | passed, logs, 0.0))
    behind = (segment == jnp.maximum(mine - 1, 0)) & (lane == jnp.where(mine == 0, 1, 0))
    scale[0] = jnp.sum(jnp.where(behind, scales, 0.0))


def product_list(index, borders, place, order, sizes, terms, half, left, seam, acc):
    chunk = seam.shape[0]
    base = index * (order.shape[0] // (len(borders) - 1))
    live = sizes[index]
    groups = (live + UNROLL - 1) // UNROLL

    def advance(opening, g, carry):
        sums = []
        for u in range(UNROLL):
            s = g * UNROLL + u
            t = order[base + s]
            e = jnp.clip(terms[0, t] - borders[index], 0, chunk - 1)
            block = left[borders[index] + e].T if opening else seam[e]
            valid = jnp.full((1, acc.shape[2]), s) < live
            sums.append((terms[3, t], jnp.where(valid, dot(block, half[t]), 0.0)))
        for o, full in sums:
            acc[o] += full
        return carry

    for opening in (False, True):

        @pl.when((place[0] == 0) == opening)
        def _():
            lax.fori_loop(0, groups, functools.partial(advance, opening), 0)


def product_first_kernel(
    place, order, sizes, terms, half, left, seam, squares, acc, passed, borders
):
    passed[...] = squares[...]

    def clear(k, carry):
        acc[k] = jnp.zeros(acc.shape[1:], jnp.float32)
        return carry

    lax.fori_loop(0, acc.shape[0], clear, 0, unroll=4)
    product_list(0, borders, place, order, sizes, terms, half, left, seam, acc)


def load_sums(acc_in, acc):
    def load(k, carry):
        acc[k] = acc_in[k]
        return carry

    lax.fori_loop(0, acc.shape[0], load, 0, unroll=4)


def product_next_kernel(
    place, order, sizes, terms, half, left, seam, squares, acc_in, acc, passed, index, borders
):
    passed[...] = squares[...]
    load_sums(acc_in, acc)
    product_list(index, borders, place, order, sizes, terms, half, left, seam, acc)


def product_last_kernel(
    place, order, sizes, terms, scale, half, left, seam, acc_in, product, acc, borders
):
    load_sums(acc_in, acc)
    index = len(borders) - 2
    product_list(index, borders, place, order, sizes, terms, half, left, seam, acc)
    inverse = 1.0 / jnp.full((1, acc.shape[2]), scale[0])

    def finish(k, carry):
        product[k] = (acc[k] * inverse).astype(jnp.bfloat16)
        return carry

    lax.fori_loop(0, acc.shape[0], finish, 0, unroll=4)


def smem():
    return pl.BlockSpec(memory_space=pltpu.SMEM)


def vmem():
    return pl.BlockSpec(memory_space=pltpu.VMEM)


def per_device(
    left_env,
    site_tensor,
    right_env,
    center,
    mpo_table,
    update_terms,
    update_count,
    heff_terms,
    heff_count,
):
    chain, mine = lax.axis_size("chain"), lax.axis_index("chain")
    place = mine.reshape(1).astype(jnp.int32)
    blocks, rows, cols = left_env.shape
    borders = (0, blocks // 4, blocks - blocks // 4, blocks)
    lists = len(borders) - 1
    update_terms, heff_terms = update_terms.T, heff_terms.T
    params = pltpu.CompilerParams(vmem_limit_bytes=VMEM_LIMIT)

    def shaped(shape, dtype):
        return jax.ShapeDtypeStruct(shape, dtype)

    def cost(microseconds):
        return pl.CostEstimate(
            flops=int(microseconds * 10**9), bytes_accessed=2**20, transcendentals=0
        )

    tile = shaped(TILE, jnp.float32)
    turned = shaped((blocks, cols, rows), jnp.bfloat16)
    pieces = [
        shaped((borders[i + 1] - borders[i], rows, cols), jnp.bfloat16) for i in range(lists)
    ]
    sums = shaped(center.shape, jnp.float32)
    lengths = shaped((lists,), jnp.int32)

    def listed(terms, dtype=jnp.int32):
        return shaped((lists * (terms.shape[1] + UNROLL),), dtype)

    def working(index):
        return [
            pltpu.VMEM((update_terms.shape[1], cols, cols), jnp.bfloat16),
            pltpu.VMEM(pieces[index].shape, jnp.float32),
        ]

    order, sizes, coefs = pl.pallas_call(
        functools.partial(list_kernel, borders=borders),
        out_shape=(listed(update_terms), lengths, listed(update_terms, jnp.float32)),
        in_specs=[smem(), smem(), smem()],
        out_specs=(smem(), smem(), smem()),
        compiler_params=params,
        cost_estimate=cost(4),
        name="list_slots",
    )(update_count, update_terms, mpo_table)

    pairs = [(k, k + 1) for k in range(chain - 1)]
    fresh, squares, site_t = pl.pallas_call(
        functools.partial(update_first_kernel, borders=borders),
        out_shape=(pieces[0], tile, turned),
        in_specs=[smem(), smem(), smem(), smem(), smem(), vmem(), vmem()],
        out_specs=(vmem(), vmem(), vmem()),
        scratch_shapes=working(0),
        compiler_params=params,
        cost_estimate=cost(5),
        name="update_first",
    )(place, order, sizes, coefs, update_terms, left_env, site_tensor)
    seams = [lax.ppermute(fresh, "chain", pairs)]
    for index in range(1, lists):
        fresh, squares = pl.pallas_call(
            functools.partial(update_next_kernel, index=index, borders=borders),
            out_shape=(pieces[index], tile),
            in_specs=[smem(), smem(), smem(), smem(), vmem(), vmem(), vmem(), vmem()],
            out_specs=(vmem(), vmem()),
            scratch_shapes=working(index),
            compiler_params=params,
            cost_estimate=cost(4),
            name="update_next",
        )(order, sizes, coefs, update_terms, left_env, site_tensor, site_t, squares)
        seams.append(lax.ppermute(fresh, "chain", pairs))

    half, order, sizes = pl.pallas_call(
        functools.partial(half_kernel, borders=borders),
        out_shape=(
            shaped((heff_terms.shape[1],) + center.shape[1:], jnp.bfloat16),
            listed(heff_terms),
            lengths,
        ),
        in_specs=[smem(), smem(), smem(), vmem(), vmem()],
        out_specs=(vmem(), smem(), smem()),
        compiler_params=params,
        cost_estimate=cost(5),
        name="half",
    )(heff_count, heff_terms, mpo_table, center, right_env)

    acc, passed = pl.pallas_call(
        functools.partial(product_first_kernel, borders=borders),
        out_shape=(sums, tile),
        in_specs=[smem(), smem(), smem(), smem(), vmem(), vmem(), vmem(), vmem()],
        out_specs=(vmem(), vmem()),
        compiler_params=params,
        cost_estimate=cost(3),
        name="product_first",
    )(place, order, sizes, heff_terms, half, left_env, seams[0], squares)
    for index in range(1, lists - 1):
        acc, passed = pl.pallas_call(
            functools.partial(product_next_kernel, index=index, borders=borders),
            out_shape=(sums, tile),
            in_specs=[smem(), smem(), smem(), smem(), vmem(), vmem(), vmem(), vmem(), vmem()],
            out_specs=(vmem(), vmem()),
            compiler_params=params,
            cost_estimate=cost(3),
            name="product_next",
        )(place, order, sizes, heff_terms, half, left_env, seams[index], passed, acc)

    number = shaped((1,), jnp.float32)
    log_scale, scale = pl.pallas_call(
        lambda *refs: exchange_kernel(float(left_env.size), *refs),
        out_shape=(number, number),
        in_specs=[vmem()],
        out_specs=(smem(), smem()),
        scratch_shapes=[
            pltpu.VMEM((chain,) + TILE, jnp.float32),
            pltpu.SemaphoreType.DMA((chain,)),
            pltpu.SemaphoreType.DMA((chain,)),
        ],
        compiler_params=pltpu.CompilerParams(
            collective_id=0, has_side_effects=True, vmem_limit_bytes=4 * 1024 * 1024
        ),
        cost_estimate=cost(3),
        name="exchange",
    )(passed)

    product = pl.pallas_call(
        functools.partial(product_last_kernel, borders=borders),
        out_shape=shaped(center.shape, jnp.bfloat16),
        in_specs=[smem(), smem(), smem(), smem(), smem(), vmem(), vmem(), vmem(), vmem()],
        out_specs=vmem(),
        scratch_shapes=[pltpu.VMEM(center.shape, jnp.float32)],
        compiler_params=params,
        cost_estimate=cost(6),
        name="product_last",
    )(place, order, sizes, heff_terms, scale, half, left_env, seams[-1], acc)
    return (product, log_scale)


def solution(mesh):
    placed = (
        P(("grp", "chain"), None, None),
        P(("grp", "chain"), None, None),
        P(("grp", "chain"), None, None),
        P(("grp", "chain"), None, None),
        P(),
        P(("grp", "chain"), None),
        P(("grp", "chain")),
        P(("grp", "chain"), None),
        P(("grp", "chain")),
    )
    return jax.shard_map(
        per_device,
        mesh=mesh,
        in_specs=placed,
        out_specs=(P(("grp", "chain"), None, None), P(("grp", "chain"))),
        check_vma=False,
    )
```

```python
import functools

import jax
import jax.numpy as jnp
from jax import lax
from jax.experimental import pallas as pl
from jax.experimental.pallas import tpu as pltpu
from jax.sharding import PartitionSpec as P

UNROLL = 16
VMEM_LIMIT = 24 * 1024 * 1024
TILE = (1, 128)


def dot(a, b):
    return jnp.dot(a, b, preferred_element_type=jnp.float32)


def sort_slots(count, keys, border, order, sizes):
    stride = order.shape[0] // 2
    live = count[0]

    def advance(g, carry):
        low, high = carry
        for u in range(UNROLL):
            t = g * UNROLL + u
            upper = (keys(t) >= border).astype(jnp.int32)
            order[jnp.where(upper == 1, stride + high, low)] = t
            valid = (t < live).astype(jnp.int32)
            low, high = low + valid * (1 - upper), high + valid * upper
        return low, high

    zero = jnp.int32(0)
    low, high = lax.fori_loop(0, (live + UNROLL - 1) // UNROLL, advance, (zero, zero))
    for u in range(UNROLL):
        order[low + u] = 0
        order[stride + high + u] = 0
    sizes[0] = low
    sizes[1] = high


def update_list(index, order, sizes, terms, table, left, site, site_t, fresh, parts, acc):
    chunk = acc.shape[0]
    base = index * (order.shape[0] // 2)
    live = sizes[index]
    groups = (live + UNROLL - 1) // UNROLL

    def clear(k, carry):
        acc[k] = jnp.zeros(acc.shape[1:], jnp.float32)
        return carry

    lax.fori_loop(0, chunk, clear, 0, unroll=4)

    def first(g, carry):
        for u in range(UNROLL):
            s = g * UNROLL + u
            t = order[base + s]
            coef = jnp.where(s < live, table[terms[4, t]], 0.0)
            part = dot(site_t[terms[1, t]], left[terms[0, t]]) * coef
            parts[s] = part.astype(jnp.bfloat16)
        return carry

    lax.fori_loop(0, groups, first, 0)

    def second(g, carry):
        sums = []
        for u in range(UNROLL):
            s = g * UNROLL + u
            t = order[base + s]
            o = terms[3, t]
            o = jnp.where(o >= chunk, o - chunk, o)
            sums.append((o, dot(parts[s], site[terms[2, t]])))
        for o, full in sums:
            acc[o] += full
        return carry

    lax.fori_loop(0, groups, second, 0)

    def finish(k, carry):
        rounded = acc[k].astype(jnp.bfloat16)
        fresh[k] = rounded if index == 0 else rounded.T
        return carry

    lax.fori_loop(0, chunk, finish, 0, unroll=4)


def list_kernel(count, terms, order, sizes, border):
    sort_slots(count, lambda t: terms[3, t], border, order, sizes)


def update_low_kernel(order, sizes, terms, table, left, site, fresh, site_t, parts, acc):
    def prepare(k, carry):
        site_t[k] = site[k].T
        return carry

    lax.fori_loop(0, left.shape[0], prepare, 0, unroll=4)
    update_list(0, order, sizes, terms, table, left, site, site_t, fresh, parts, acc)


def update_high_kernel(order, sizes, terms, table, left, site, site_t, fresh, parts, acc):
    update_list(1, order, sizes, terms, table, left, site, site_t, fresh, parts, acc)


def sum_squares(blocks):
    def add(k, total):
        wide = blocks[k].astype(jnp.float32)
        return total + wide * wide

    zero = jnp.zeros(blocks.shape[1:], jnp.float32)
    return jnp.sum(lax.fori_loop(0, blocks.shape[0], add, zero, unroll=4))


def half_kernel(
    place, count, terms, table, center, right, left, low, high,
    half, order, sizes, squares, border,
):
    lane = lax.broadcasted_iota(jnp.int32, TILE, 1)
    squares[...] = jnp.where(lane == 0, sum_squares(low) + sum_squares(high), 0.0)

    @pl.when(place[0] == 0)
    def _():
        squares[...] = jnp.where(lane == 1, sum_squares(left), squares[...])

    sort_slots(count, lambda t: terms[0, t], border, order, sizes)

    def advance(g, carry):
        for u in range(UNROLL):
            t = g * UNROLL + u
            coef = jnp.where(t < count[0], table[terms[4, t]] * table[terms[5, t]], 0.0)
            value = dot(center[terms[1, t]], right[terms[2, t]]) * coef
            half[t] = value.astype(jnp.bfloat16)
        return carry

    lax.fori_loop(0, (count[0] + UNROLL - 1) // UNROLL, advance, 0)


def exchange_kernel(size, squares, log_scale, scale, held, send_sem, recv_sem):
    chain, mine = held.shape[0], lax.axis_index("chain")
    held[...] = jnp.zeros(held.shape, jnp.float32)
    held[mine] = squares[...]
    barrier = pltpu.get_barrier_semaphore()

    def copy(source, target):
        return pltpu.make_async_remote_copy(
            src_ref=squares,
            dst_ref=held.at[source],
            send_sem=send_sem.at[target],
            recv_sem=recv_sem.at[source],
            device_id={"chain": target},
            device_id_type=pl.DeviceIdType.MESH,
        )

    def greet(k, carry):
        @pl.when(k != mine)
        def _():
            pl.semaphore_signal(
                barrier, inc=1, device_id={"chain": k}, device_id_type=pl.DeviceIdType.MESH
            )

        return carry

    lax.fori_loop(0, chain, greet, 0)
    pl.semaphore_wait(barrier, chain - 1)

    def send(k, carry):
        copy(mine, k).start()
        return carry

    def sent(k, carry):
        copy(mine, k).wait_send()
        return carry

    def arrived(k, carry):
        copy(k, mine).wait_recv()
        return carry

    lax.fori_loop(mine + 1, chain, send, 0)
    lax.fori_loop(0, mine, arrived, 0)
    lax.fori_loop(mine + 1, chain, sent, 0)
    scales = jnp.sqrt(held[...] / size + 1e-06)
    logs = jnp.log(scales)
    segment = lax.broadcasted_iota(jnp.int32, held.shape, 0)
    lane = lax.broadcasted_iota(jnp.int32, held.shape, 2)
    opening = (segment == 0) & (lane == 1)
    passed = (segment < mine) & (lane == 0)
    log_scale[0] = jnp.sum(jnp.where(opening | passed, logs, 0.0))
    behind = (segment == jnp.maximum(mine - 1, 0)) & (lane == jnp.where(mine == 0, 1, 0))
    scale[0] = jnp.sum(jnp.where(behind, scales, 0.0))


def product_list(index, place, order, sizes, terms, half, left, seam, acc):
    chunk = seam.shape[0]
    base = index * (order.shape[0] // 2)
    live = sizes[index]
    groups = (live + UNROLL - 1) // UNROLL

    def advance(opening, g, carry):
        sums = []
        for u in range(UNROLL):
            s = g * UNROLL + u
            t = order[base + s]
            e = terms[0, t]
            e = jnp.where(e >= chunk, e - chunk, e)
            block = left[index * chunk + e].T if opening else seam[e]
            valid = jnp.full((1, acc.shape[2]), s) < live
            sums.append((terms[3, t], jnp.where(valid, dot(block, half[t]), 0.0)))
        for o, full in sums:
            acc[o] += full
        return carry

    for opening in (False, True):

        @pl.when((place[0] == 0) == opening)
        def _():
            lax.fori_loop(0, groups, functools.partial(advance, opening), 0)


def product_low_kernel(
    place, order, sizes, terms, half, left, seam, squares, acc, passed, seam_t
):
    passed[...] = squares[...]

    def turn(k, carry):
        seam_t[k] = seam[k].T
        return carry

    lax.fori_loop(0, seam.shape[0], turn, 0, unroll=4)

    def clear(k, carry):
        acc[k] = jnp.zeros(acc.shape[1:], jnp.float32)
        return carry

    lax.fori_loop(0, acc.shape[0], clear, 0, unroll=4)
    product_list(0, place, order, sizes, terms, half, left, seam_t, acc)


def product_high_kernel(place, order, sizes, terms, scale, half, left, seam, acc_in, product, acc):
    def load(k, carry):
        acc[k] = acc_in[k]
        return carry

    lax.fori_loop(0, acc.shape[0], load, 0, unroll=4)
    product_list(1, place, order, sizes, terms, half, left, seam, acc)
    inverse = 1.0 / jnp.full((1, acc.shape[2]), scale[0])

    def finish(k, carry):
        product[k] = (acc[k] * inverse).astype(jnp.bfloat16)
        return carry

    lax.fori_loop(0, acc.shape[0], finish, 0, unroll=4)


def smem():
    return pl.BlockSpec(memory_space=pltpu.SMEM)


def vmem():
    return pl.BlockSpec(memory_space=pltpu.VMEM)


def per_device(
    left_env,
    site_tensor,
    right_env,
    center,
    mpo_table,
    update_terms,
    update_count,
    heff_terms,
    heff_count,
):
    chain, mine = lax.axis_size("chain"), lax.axis_index("chain")
    place = mine.reshape(1).astype(jnp.int32)
    blocks, rows, cols = left_env.shape
    chunk = blocks // 2
    update_terms, heff_terms = update_terms.T, heff_terms.T
    params = pltpu.CompilerParams(vmem_limit_bytes=VMEM_LIMIT)

    def shaped(shape, dtype):
        return jax.ShapeDtypeStruct(shape, dtype)

    def cost(microseconds):
        return pl.CostEstimate(
            flops=int(microseconds * 10**9), bytes_accessed=2**20, transcendentals=0
        )

    tile = shaped(TILE, jnp.float32)
    turned = shaped((blocks, cols, rows), jnp.bfloat16)
    piece = shaped((chunk, rows, cols), jnp.bfloat16)
    sums = shaped(center.shape, jnp.float32)
    two = shaped((2,), jnp.int32)

    def listed(terms, dtype=jnp.int32):
        return shaped((2 * (terms.shape[1] + UNROLL),), dtype)

    working = [
        pltpu.VMEM((update_terms.shape[1], cols, cols), jnp.bfloat16),
        pltpu.VMEM((chunk, cols, cols), jnp.float32),
    ]
    order, sizes = pl.pallas_call(
        functools.partial(list_kernel, border=chunk),
        out_shape=(listed(update_terms), two),
        in_specs=[smem(), smem()],
        out_specs=(smem(), smem()),
        compiler_params=params,
        cost_estimate=cost(4),
        name="list_slots",
    )(update_count, update_terms)

    low, site_t = pl.pallas_call(
        update_low_kernel,
        out_shape=(piece, turned),
        in_specs=[smem(), smem(), smem(), smem(), vmem(), vmem()],
        out_specs=(vmem(), vmem()),
        scratch_shapes=working,
        compiler_params=params,
        cost_estimate=cost(9),
        name="update_low",
    )(order, sizes, update_terms, mpo_table, left_env, site_tensor)
    pairs = [(k, k + 1) for k in range(chain - 1)]
    seam_low = lax.ppermute(low, "chain", pairs)

    high = pl.pallas_call(
        update_high_kernel,
        out_shape=piece,
        in_specs=[smem(), smem(), smem(), smem(), vmem(), vmem(), vmem()],
        out_specs=vmem(),
        scratch_shapes=working,
        compiler_params=params,
        cost_estimate=cost(5),
        name="update_high",
    )(order, sizes, update_terms, mpo_table, left_env, site_tensor, site_t)
    seam_high = lax.ppermute(high, "chain", pairs)

    half, order, sizes, squares = pl.pallas_call(
        functools.partial(half_kernel, border=chunk),
        out_shape=(
            shaped((heff_terms.shape[1],) + center.shape[1:], jnp.bfloat16),
            listed(heff_terms),
            two,
            tile,
        ),
        in_specs=[smem(), smem(), smem(), smem(), vmem(), vmem(), vmem(), vmem(), vmem()],
        out_specs=(vmem(), smem(), smem(), vmem()),
        compiler_params=params,
        cost_estimate=cost(5),
        name="half",
    )(place, heff_count, heff_terms, mpo_table, center, right_env, left_env, low, high)

    acc, passed = pl.pallas_call(
        product_low_kernel,
        out_shape=(sums, tile),
        in_specs=[smem(), smem(), smem(), smem(), vmem(), vmem(), vmem(), vmem()],
        out_specs=(vmem(), vmem()),
        scratch_shapes=[pltpu.VMEM((chunk, cols, rows), jnp.bfloat16)],
        compiler_params=params,
        cost_estimate=cost(4),
        name="product_low",
    )(place, order, sizes, heff_terms, half, left_env, seam_low, squares)

    number = shaped((1,), jnp.float32)
    log_scale, scale = pl.pallas_call(
        lambda *refs: exchange_kernel(float(left_env.size), *refs),
        out_shape=(number, number),
        in_specs=[vmem()],
        out_specs=(smem(), smem()),
        scratch_shapes=[
            pltpu.VMEM((chain,) + TILE, jnp.float32),
            pltpu.SemaphoreType.DMA((chain,)),
            pltpu.SemaphoreType.DMA((chain,)),
        ],
        compiler_params=pltpu.CompilerParams(
            collective_id=0, has_side_effects=True, vmem_limit_bytes=4 * 1024 * 1024
        ),
        cost_estimate=cost(3),
        name="exchange",
    )(passed)

    product = pl.pallas_call(
        product_high_kernel,
        out_shape=shaped(center.shape, jnp.bfloat16),
        in_specs=[smem(), smem(), smem(), smem(), smem(), vmem(), vmem(), vmem(), vmem()],
        out_specs=vmem(),
        scratch_shapes=[pltpu.VMEM(center.shape, jnp.float32)],
        compiler_params=params,
        cost_estimate=cost(6),
        name="product_high",
    )(place, order, sizes, heff_terms, scale, half, left_env, seam_high, acc)
    return (product, log_scale)


def solution(mesh):
    placed = (
        P(("grp", "chain"), None, None),
        P(("grp", "chain"), None, None),
        P(("grp", "chain"), None, None),
        P(("grp", "chain"), None, None),
        P(),
        P(("grp", "chain"), None),
        P(("grp", "chain")),
        P(("grp", "chain"), None),
        P(("grp", "chain")),
    )
    return jax.shard_map(
        per_device,
        mesh=mesh,
        in_specs=placed,
        out_specs=(P(("grp", "chain"), None, None), P(("grp", "chain"))),
        check_vma=False,
    )
```
